32 devices in a mesh: grp: 2 (over y), gx: 16 (over z, x, core).
Axes of the slice: x: 2, y: 2, z: 4, core: 2. Of those that a mesh axis runs over, the one named last changes fastest.
Arguments:
- volume: float32 [512, 896], P(('grp', 'gx')), parts along dimension 0, may hold values from -45 to 45
- bank: float32 [8, 4096], P(None, 'gx'), may hold values from -43 to 43
- orient: int32 [8], replicated, may hold values from 0 to 47
- bank_id: int32 [8], replicated, may hold values from 0 to 7, each once
- counts: int32 [8], replicated, may hold values from 1 to 16
Outputs:
- fields: float32 [4, 512, 896], P(None, ('grp', 'gx')), parts along dimension 1
The draws below stay inside these ranges and needn't reach their ends.
There are 2 independent parts, one for each index of `grp`. The reference program is written for one: setup_inputs(seed, part) draws one part's arguments, and reference() takes and returns one part's arrays. A program takes and returns all parts, laid end to end along the dimension named above; an argument that names none is the same for every part. Nothing has to cross between parts.
Inputs may be any that keep to these rules, and one draw needn't show every extreme that they name: `bank_id`: each of the 8 base templates is named by exactly one list entry.
All inputs are finite; a program needn't handle non-finite values.
Results may differ from the reference program's by a relative error of at most 0.0003.
Values sent between devices are 32-bit elements; how exact they have to be, the bound alone decides.
A program may use at most 64 MiB of HBM per device.

```python
import math
import jax
import jax.numpy as jnp
import numpy as np
from jax import lax

BY = 8
BZ = 112
TS = 16
NT = 8
FIELDS = 4
PER = 2
NX = 256


def draw_volume(key, part):
    keys_all = jax.random.split(jax.random.fold_in(key, 11), 3)
    columns = BY * BZ
    row_scale = jnp.exp(jax.random.uniform(keys_all[1], (NX, 1), jnp.float32, 0.0, math.log(3.2)))
    col_scale = jnp.exp(jax.random.uniform(keys_all[2], (1, columns), jnp.float32, 0.0, math.log(3.2)))
    noise = jnp.clip(jax.random.normal(keys_all[0], (NX, columns), jnp.float32), -4.0, 4.0)
    return noise * row_scale * col_scale


def draw_bank(key, part):
    keys_all = jax.random.split(jax.random.fold_in(key, 23), 2)
    voxels = TS * TS * TS
    voxel_scale = jnp.exp(jax.random.uniform(keys_all[1], (NT, voxels), jnp.float32, 0.0, math.log(10.0)))
    noise = jnp.clip(jax.random.normal(keys_all[0], (NT, voxels), jnp.float32), -4.0, 4.0)
    return noise * voxel_scale


def touch_ends(entries, own_key, low, largest):
    index_at = [jax.random.randint(jax.random.fold_in(own_key, axis), (), 0, length) for axis, length in enumerate(entries.shape)]
    widest = entries.shape.index(max(entries.shape))
    neighbour = index_at[:widest] + [(index_at[widest] + 1) % entries.shape[widest]] + index_at[widest + 1:]
    return entries.at[tuple(index_at)].set(low).at[tuple(neighbour)].set(largest)


def setup_inputs(seed: int = 0, part: int = 0) -> dict:
    seeds = jax.random.split(jax.random.key(seed), 6)
    part_splits = jax.random.split(jax.random.fold_in(seeds[5], part), 6)
    return {
        "volume": draw_volume(jax.random.fold_in(jax.random.fold_in(seeds[5], part), 71), part),
        "bank": draw_bank(jax.random.fold_in(seeds[5], 71), part),
        "orient": touch_ends(jax.random.randint(seeds[2], (NT,), 0, 48), jax.random.fold_in(seeds[2], 1), 0, 47).astype(jnp.int32),
        "bank_id": jax.random.permutation(seeds[3], NT).astype(jnp.int32),
        "counts": touch_ends(jax.random.randint(seeds[4], (NT,), 1, 17), jax.random.fold_in(seeds[4], 1), 1, 16).astype(jnp.int32),
    }


epsilon = 1e-05
sharpness = 80.0
AXIS_ORDERS = np.array([[0, 1, 2], [0, 2, 1], [1, 0, 2], [1, 2, 0], [2, 0, 1], [2, 1, 0]], np.int32)

def rotate_template(flat_base, orient_one):
    coords = jnp.arange(TS ** 3, dtype=jnp.int32)
    index_set = jnp.stack([coords // (TS * TS), coords // TS % TS, coords % TS])
    order_row = orient_one // 8
    flip_set = orient_one % 8
    picked = (jnp.arange(6, dtype=jnp.int32) == order_row).astype(jnp.int32)
    ordering = lax.optimization_barrier(jnp.sum(picked[:, None] * jnp.asarray(AXIS_ORDERS), axis=0))
    source = jnp.zeros_like(coords)
    for axis_num in range(3):
        select = (ordering[axis_num] == jnp.arange(3, dtype=jnp.int32)).astype(jnp.int32)
        chosen = lax.optimization_barrier(jnp.sum(select[:, None] * index_set, axis=0))
        flipped = flip_set // 2 ** axis_num % 2
        placed = chosen + flipped * (TS - 1 - 2 * chosen)
        source = source * TS + placed
    return flat_base[source]

def normalized_kernel(flat_base, orient_one):
    rotated = rotate_template(flat_base, orient_one)
    centered = rotated - jnp.mean(rotated)
    return centered / jnp.sqrt(jnp.sum(centered * centered) + epsilon)

def reference(volume, bank, orient, bank_id, counts):
    half = TS // 2
    grid = volume.reshape(NX, BY, BZ)
    padded = jnp.pad(grid, ((half, TS - half), (half, TS - half), (half, TS - half)))
    full_shape = padded.shape
    spectrum = jnp.fft.rfftn(padded)

    def one_template(entry):
        flat_base = bank[bank_id[entry]]
        kernel = normalized_kernel(flat_base, orient[entry]).reshape(TS, TS, TS)
        kernel_spec = jnp.fft.rfftn(kernel, s=full_shape)
        product = jnp.fft.irfftn(spectrum * jnp.conj(kernel_spec), s=full_shape)
        return product[:NX, :BY, :BZ]
    numer = lax.map(one_template, jnp.arange(NT, dtype=jnp.int32))
    squares = padded * padded
    for axis_num in range(3):
        window = [1, 1, 1]
        window[axis_num] = TS
        squares = lax.reduce_window(squares, jnp.array(0, squares.dtype), lax.add, tuple(window), (1, 1, 1), 'VALID')
    energy = squares[:NX, :BY, :BZ]
    scores = numer / jnp.sqrt(energy + epsilon)[None]
    weights = counts.astype(jnp.float32)
    weighted = weights[:, None, None, None] * jnp.exp(sharpness * scores)
    grouped = lax.optimization_barrier(jnp.sum(weighted.reshape(FIELDS, PER, NX, BY, BZ), axis=1))
    totals = lax.optimization_barrier(jnp.sum(weights.reshape(FIELDS, PER), axis=1))
    fields = jnp.log(grouped / totals[:, None, None, None])
    return fields.reshape(FIELDS, NX, BY * BZ)
```

```python
import functools

import jax
import jax.numpy as jnp
from jax import lax
from jax.experimental import pallas as pl
from jax.experimental.pallas import tpu as pltpu
from jax.sharding import PartitionSpec as P

BY = 8
BZ = 112
TS = 16
NT = 8
FIELDS = 4
PER = NT // FIELDS
ROWS = 16
EXT = ROWS + TS
LANES = 128
KB = TS * EXT
HALF = TS // 2
MESH = pl.DeviceIdType.MESH

epsilon = 1e-05
sharpness = 80.0
f32 = jnp.float32
bf16 = jnp.bfloat16


def lane_iota(shape):
    return lax.broadcasted_iota(jnp.int32, shape, len(shape) - 1)


def swap_bit(tiles, bit, dist, lane):
    out = list(tiles)
    low = (lane & dist) == 0
    for i in range(TS):
        if i & (1 << bit):
            continue
        j = i | (1 << bit)
        for h in range(2):
            a, b = tiles[i][h], tiles[j][h]
            na = jnp.where(low, a, pltpu.roll(b, dist, 1))
            nb = jnp.where(low, pltpu.roll(a, LANES - dist, 1), b)
            out[i] = [na if g == h else out[i][g] for g in range(2)]
            out[j] = [nb if g == h else out[j][g] for g in range(2)]
    return out


def swap_high(tiles):
    out = [None] * TS
    for i in range(TS):
        top = i >> 3
        out[i] = [tiles[(i & 7) | (h << 3)][top] for h in range(2)]
    return out


def kernel(n, gather, orient, bank_id, counts, vol, bank, out, sendbuf, slots, ext, pst, wst, hot, lhs, rot,
           bsend, brecv, hsend, hrecv):
    me = lax.axis_index("gx")
    has_left = me > 0
    has_right = me < n - 1
    left = jnp.maximum(me - 1, 0)
    right = jnp.minimum(me + 1, n - 1)

    barrier = pltpu.get_barrier_semaphore()
    if gather:
        for k in range(1, n):
            pl.semaphore_signal(barrier, inc=1, device_id={"gx": lax.rem(me + k, n)}, device_id_type=MESH)
    else:
        @pl.when(has_left)
        def _():
            pl.semaphore_signal(barrier, inc=1, device_id={"gx": left}, device_id_type=MESH)

        @pl.when(has_right)
        def _():
            pl.semaphore_signal(barrier, inc=1, device_id={"gx": right}, device_id_type=MESH)

    if gather:
        for t in range(NT):
            sendbuf[t:t + 1, :] = bank[pl.ds(bank_id[t], 1), :]
        slots[me] = sendbuf[...]
        pl.semaphore_wait(barrier, n - 1)
    else:
        slots[...] = bank[...]

        @pl.when(has_left)
        def _():
            pl.semaphore_wait(barrier, 1)

        @pl.when(has_right)
        def _():
            pl.semaphore_wait(barrier, 1)

    to_right = pltpu.make_async_remote_copy(
        src_ref=vol.at[pl.ds(ROWS - HALF, HALF)], dst_ref=ext.at[pl.ds(0, HALF)],
        send_sem=hsend.at[0], recv_sem=hrecv.at[0], device_id={"gx": right}, device_id_type=MESH)
    to_left = pltpu.make_async_remote_copy(
        src_ref=vol.at[pl.ds(0, HALF)], dst_ref=ext.at[pl.ds(HALF + ROWS, HALF)],
        send_sem=hsend.at[1], recv_sem=hrecv.at[1], device_id={"gx": left}, device_id_type=MESH)

    @pl.when(has_right)
    def _():
        to_right.start()

    @pl.when(has_left)
    def _():
        to_left.start()

    sends = []
    if gather:
        for k in range(1, n):
            copy = pltpu.make_async_remote_copy(
                src_ref=sendbuf, dst_ref=slots.at[me], send_sem=bsend.at[k], recv_sem=brecv.at[k],
                device_id={"gx": lax.rem(me + k, n)}, device_id_type=MESH)
            copy.start()
            sends.append(copy)

    ext[pl.ds(HALF, ROWS), :] = vol[...]

    @pl.when(jnp.logical_not(has_left))
    def _():
        ext[pl.ds(0, HALF), :] = jnp.zeros((HALF, BY * BZ), f32)

    @pl.when(jnp.logical_not(has_right))
    def _():
        ext[pl.ds(HALF + ROWS, HALF), :] = jnp.zeros((HALF, BY * BZ), f32)

    wide = (TS * TS, KB)
    lane = lane_iota((1, KB))
    c_of, a_of = lane >> 5, lane & 31
    row = lax.broadcasted_iota(jnp.int32, wide, 0)
    for g in range(8):
        u = a_of if g & 4 else c_of
        v = c_of if g & 4 else a_of
        u = (TS - 1 - u) if g & 2 else u
        v = (TS - 1 - v) if g & 1 else v
        source = jnp.where(a_of < TS, u * TS + v, -1)
        hot[pl.ds(g * TS * TS, TS * TS), :] = jnp.where(row == source, 1.0, 0.0).astype(bf16)

    @pl.when(has_left)
    def _():
        to_right.wait_recv()

    @pl.when(has_right)
    def _():
        to_left.wait_recv()

    zl = lane_iota((EXT, LANES))
    total = None
    for y in range(BY):
        if y == 0:
            value = ext[:, pl.ds(0, LANES)]
        else:
            value = pltpu.roll(ext[:, pl.ds((y - 1) * LANES, LANES)], TS * y, 1)
            if y < BY - 1:
                value = jnp.where(zl < TS * y, value, pltpu.roll(ext[:, pl.ds(y * LANES, LANES)], TS * y, 1))
        value = jnp.where(zl < BZ, value, 0.0)
        square = value * value
        total = square if total is None else total + square
        for c in range(TS):
            shifted = value if c == HALF else pltpu.roll(value, (HALF - c) % LANES, 1)
            high = shifted.astype(bf16)
            low = (shifted - high.astype(f32)).astype(bf16)
            rows = pl.ds((y * TS + c) * EXT, EXT)
            pst[rows, pl.ds(0, LANES)] = high
            pst[rows, pl.ds(LANES, LANES)] = low
    for step in (1, 2, 4, 8):
        total = total + pltpu.roll(total, LANES - step, 1)
    total = pltpu.roll(total, HALF, 1)
    for step in (1, 2, 4, 8):
        total = total + pltpu.roll(total, EXT - step, 0)
    scale = sharpness * lax.rsqrt(total[:ROWS] + epsilon)

    if gather:
        for k in range(1, n):
            pltpu.make_async_remote_copy(
                src_ref=sendbuf, dst_ref=slots.at[lax.rem(me + n - k, n)], send_sem=bsend.at[k],
                recv_sem=brecv.at[k], device_id={"gx": lax.rem(me + k, n)}, device_id_type=MESH).wait_recv()

    tile = (NT, LANES)
    zero = [[slots[i, :, pl.ds(h * LANES, LANES)] for h in range(2)] for i in range(TS)]
    acc = functools.reduce(jnp.add, [x for pair in zero for x in pair])
    mean = jnp.sum(acc, axis=1, keepdims=True) * (1.0 / TS**3)
    zero = [[x - mean for x in pair] for pair in zero]
    acc = functools.reduce(jnp.add, [x * x for pair in zero for x in pair])
    inv = lax.rsqrt(jnp.sum(acc, axis=1, keepdims=True) + epsilon)
    zero = [[x * inv for x in pair] for pair in zero]

    tl = lane_iota(tile)
    one = swap_high(zero)
    for bit, dist in ((2, 64), (1, 32), (0, 16)):
        one = swap_bit(one, bit, dist, tl)
    two = zero
    for bit, dist in ((3, 8), (2, 4), (1, 2), (0, 1)):
        two = swap_bit(two, bit, dist, tl)

    sub = lax.broadcasted_iota(jnp.int32, tile, 0)
    o = jnp.zeros(tile, jnp.int32)
    for t in range(NT):
        o = jnp.where(sub == t, orient[t], o)
    p = o >> 3
    bit0, bit1, bit2 = o & 1, (o >> 1) & 1, (o >> 2) & 1
    rows0 = (p == 2) | (p == 3)
    rows1 = (p == 0) | (p == 5)
    flip_b = jnp.where(rows0, bit0, jnp.where(rows1, bit1, bit2)) == 1
    flip_u = jnp.where(rows1, bit0, bit1)
    flip_v = jnp.where(rows0 | rows1, bit2, bit0)
    which = (1 - (p & 1)) * 4 + flip_u * 2 + flip_v
    picked = [[jnp.where(rows0, zero[i][h], jnp.where(rows1, one[i][h], two[i][h])) for h in range(2)]
              for i in range(TS)]
    picked = [[jnp.where(flip_b, picked[TS - 1 - i][h], picked[i][h]) for h in range(2)] for i in range(TS)]
    which = jnp.concatenate([which, which], axis=0)
    for i in range(0, TS, 2):
        for h in range(2):
            both = jnp.concatenate([picked[i][h], picked[i + 1][h]], axis=0)
            high = both.astype(bf16).astype(f32)
            low = both - high
            for g in range(8):
                cols = pl.ds(g * TS * TS + h * LANES, LANES)
                lhs[pl.ds(i * NT, 2 * NT), cols] = jnp.where(which == g, high, 0.0).astype(bf16)
                lhs[pl.ds(TS * NT + i * NT, 2 * NT), cols] = jnp.where(which == g, low, 0.0).astype(bf16)
    turned = jnp.dot(lhs[...], hot[...], preferred_element_type=f32)
    rot[...] = turned[:TS * NT] + turned[TS * NT:]

    def band(b, carry):
        for j in range(KB // LANES):
            lines = rot[pl.ds(pl.multiple_of(b * NT, NT), NT), pl.ds(j * LANES, LANES)]
            for t in range(NT):
                line = jnp.broadcast_to(lines[t:t + 1], (ROWS, LANES))
                line = pltpu.roll(line, 0, 1, stride=1, stride_axis=0)
                high = line.astype(bf16)
                low = (line - high.astype(f32)).astype(bf16)
                cols = pl.ds(pl.multiple_of((b - 1) * KB + j * LANES, LANES), LANES)
                wst[pl.ds(t * ROWS, ROWS), cols] = high
                wst[pl.ds((NT + t) * ROWS, ROWS), cols] = low
        return carry

    lax.fori_loop(1, TS, band, 0)

    weights = []
    for k in range(FIELDS):
        parts = [jnp.full((ROWS, LANES), counts[k * PER + i].astype(f32)) for i in range(PER)]
        whole = functools.reduce(jnp.add, parts)
        weights.append([x / whole for x in parts])
    ol = lane_iota((ROWS, LANES))
    half_m = NT * ROWS
    before = [None] * FIELDS
    for y in range(BY):
        res = jnp.dot(wst[:, pl.ds((BY - 1 - y) * KB, BY * KB)], pst[...], preferred_element_type=f32)
        numer = (res[:half_m, :LANES] + (res[:half_m, LANES:] + res[half_m:, :LANES])) + res[half_m:, LANES:]
        for k in range(FIELDS):
            value = None
            for i in range(PER):
                t = k * PER + i
                term = weights[k][i] * jnp.exp(numer[t * ROWS:(t + 1) * ROWS] * scale)
                value = term if value is None else value + term
            value = jnp.log(value)
            if y:
                value = pltpu.roll(value, LANES - TS * y, 1)
                out[k, :, pl.ds((y - 1) * LANES, LANES)] = jnp.where(ol < BZ - TS * (y - 1), before[k], value)
            before[k] = value

    if gather:
        for copy in sends:
            copy.wait_send()

    @pl.when(has_right)
    def _():
        to_right.wait_send()

    @pl.when(has_left)
    def _():
        to_left.wait_send()


def local(n, volume, bank, orient, bank_id, counts):
    gather = bank.shape[1] == TS * TS
    if not gather:
        whole = lax.all_gather(bank, "gx", axis=1, tiled=True)[bank_id]
        bank = whole.reshape(NT, TS, TS * TS).transpose(1, 0, 2)
    smem = pl.BlockSpec(memory_space=pltpu.SMEM)
    vmem = pl.BlockSpec(memory_space=pltpu.VMEM)
    return pl.pallas_call(
        functools.partial(kernel, n, gather),
        out_shape=jax.ShapeDtypeStruct((FIELDS, ROWS, BY * BZ), f32),
        in_specs=[smem, smem, smem, vmem, vmem],
        out_specs=vmem,
        scratch_shapes=[
            pltpu.VMEM((NT, TS * TS), f32),
            pltpu.VMEM((TS, NT, TS * TS), f32),
            pltpu.VMEM((EXT, BY * BZ), f32),
            pltpu.VMEM((BY * KB, 2 * LANES), bf16),
            pltpu.VMEM((2 * NT * ROWS, (TS - 1) * KB), bf16),
            pltpu.VMEM((8 * TS * TS, KB), bf16),
            pltpu.VMEM((2 * TS * NT, 8 * TS * TS), bf16),
            pltpu.VMEM((TS * NT, KB), f32),
            pltpu.SemaphoreType.DMA((TS,)),
            pltpu.SemaphoreType.DMA((TS,)),
            pltpu.SemaphoreType.DMA((2,)),
            pltpu.SemaphoreType.DMA((2,)),
        ],
        compiler_params=pltpu.CompilerParams(
            collective_id=0, has_side_effects=True, vmem_limit_bytes=40 * 1024 * 1024),
        cost_estimate=pl.CostEstimate(flops=4_000_000_000, bytes_accessed=400_000, transcendentals=200_000),
    )(orient, bank_id, counts, volume, bank)


def solution(mesh):
    in_specs = (P(("grp", "gx"), None), P(None, "gx"), P(), P(), P())
    out_specs = P(None, ("grp", "gx"), None)
    return jax.shard_map(functools.partial(local, mesh.shape["gx"]), mesh=mesh, in_specs=in_specs,
                         out_specs=out_specs, check_vma=False)
```

```python
import functools

import jax
import jax.numpy as jnp
from jax import lax
from jax.experimental import pallas as pl
from jax.experimental.pallas import tpu as pltpu
from jax.sharding import PartitionSpec as P

BY = 8
BZ = 112
TS = 16
NT = 8
FIELDS = 4
PER = NT // FIELDS
ROWS = 16
EXT = ROWS + TS
LANES = 128
KB = TS * EXT
HALF = TS // 2
MESH = pl.DeviceIdType.MESH

epsilon = 1e-05
sharpness = 80.0
f32 = jnp.float32
bf16 = jnp.bfloat16


def lane_iota(shape):
    return lax.broadcasted_iota(jnp.int32, shape, len(shape) - 1)


def swap_bit(tiles, bit, dist, lane):
    out = list(tiles)
    low = (lane & dist) == 0
    for i in range(TS):
        if i & (1 << bit):
            continue
        j = i | (1 << bit)
        for h in range(2):
            a, b = tiles[i][h], tiles[j][h]
            na = jnp.where(low, a, pltpu.roll(b, dist, 1))
            nb = jnp.where(low, pltpu.roll(a, LANES - dist, 1), b)
            out[i] = [na if g == h else out[i][g] for g in range(2)]
            out[j] = [nb if g == h else out[j][g] for g in range(2)]
    return out


def swap_high(tiles):
    out = [None] * TS
    for i in range(TS):
        top = i >> 3
        out[i] = [tiles[(i & 7) | (h << 3)][top] for h in range(2)]
    return out


def kernel(n, gather, orient_in, bank_id_in, counts_in, vol_in, bank_in, out, orient, bank_id, counts, vol, bank,
           sendbuf, slots, ext, pst, wst, hot, lhs, rot, fetch, bsend, brecv, hsend, hrecv):
    pairs = ((vol_in, vol), (bank_id_in, bank_id), (bank_in, bank), (orient_in, orient), (counts_in, counts))
    fetches = [pltpu.make_async_copy(src, dst, fetch.at[i]) for i, (src, dst) in enumerate(pairs)]
    for copy in fetches:
        copy.start()
    me = lax.axis_index("gx")
    has_left = me > 0
    has_right = me < n - 1
    left = jnp.maximum(me - 1, 0)
    right = jnp.minimum(me + 1, n - 1)

    barrier = pltpu.get_barrier_semaphore()
    if gather:
        for k in range(1, n):
            pl.semaphore_signal(barrier, inc=1, device_id={"gx": lax.rem(me + k, n)}, device_id_type=MESH)
    else:
        @pl.when(has_left)
        def _():
            pl.semaphore_signal(barrier, inc=1, device_id={"gx": left}, device_id_type=MESH)

        @pl.when(has_right)
        def _():
            pl.semaphore_signal(barrier, inc=1, device_id={"gx": right}, device_id_type=MESH)

    for copy in fetches:
        copy.wait()
    if gather:
        for t in range(NT):
            sendbuf[t:t + 1, :] = bank[pl.ds(bank_id[t], 1), :]
        slots[me] = sendbuf[...]
        pl.semaphore_wait(barrier, n - 1)
    else:
        slots[...] = bank[...]

        @pl.when(has_left)
        def _():
            pl.semaphore_wait(barrier, 1)

        @pl.when(has_right)
        def _():
            pl.semaphore_wait(barrier, 1)

    to_right = pltpu.make_async_remote_copy(
        src_ref=vol.at[pl.ds(ROWS - HALF, HALF)], dst_ref=ext.at[pl.ds(0, HALF)],
        send_sem=hsend.at[0], recv_sem=hrecv.at[0], device_id={"gx": right}, device_id_type=MESH)
    to_left = pltpu.make_async_remote_copy(
        src_ref=vol.at[pl.ds(0, HALF)], dst_ref=ext.at[pl.ds(HALF + ROWS, HALF)],
        send_sem=hsend.at[1], recv_sem=hrecv.at[1], device_id={"gx": left}, device_id_type=MESH)

    @pl.when(has_right)
    def _():
        to_right.start()

    @pl.when(has_left)
    def _():
        to_left.start()

    sends = []
    if gather:
        for k in range(1, n):
            copy = pltpu.make_async_remote_copy(
                src_ref=sendbuf, dst_ref=slots.at[me], send_sem=bsend.at[k], recv_sem=brecv.at[k],
                device_id={"gx": lax.rem(me + k, n)}, device_id_type=MESH)
            copy.start()
            sends.append(copy)

    ext[pl.ds(HALF, ROWS), :] = vol[...]

    @pl.when(jnp.logical_not(has_left))
    def _():
        ext[pl.ds(0, HALF), :] = jnp.zeros((HALF, BY * BZ), f32)

    @pl.when(jnp.logical_not(has_right))
    def _():
        ext[pl.ds(HALF + ROWS, HALF), :] = jnp.zeros((HALF, BY * BZ), f32)

    wide = (TS * TS, KB)
    lane = lane_iota((1, KB))
    c_of, a_of = lane >> 5, lane & 31
    row = lax.broadcasted_iota(jnp.int32, wide, 0)
    for g in range(8):
        u = a_of if g & 4 else c_of
        v = c_of if g & 4 else a_of
        u = (TS - 1 - u) if g & 2 else u
        v = (TS - 1 - v) if g & 1 else v
        source = jnp.where(a_of < TS, u * TS + v, -1)
        hot[pl.ds(g * TS * TS, TS * TS), :] = jnp.where(row == source, 1.0, 0.0).astype(bf16)

    @pl.when(has_left)
    def _():
        to_right.wait_recv()

    @pl.when(has_right)
    def _():
        to_left.wait_recv()

    zl = lane_iota((EXT, LANES))
    total = None
    for y in range(BY):
        if y == 0:
            value = ext[:, pl.ds(0, LANES)]
        else:
            value = pltpu.roll(ext[:, pl.ds((y - 1) * LANES, LANES)], TS * y, 1)
            if y < BY - 1:
                value = jnp.where(zl < TS * y, value, pltpu.roll(ext[:, pl.ds(y * LANES, LANES)], TS * y, 1))
        value = jnp.where(zl < BZ, value, 0.0)
        square = value * value
        total = square if total is None else total + square
        for c in range(TS):
            shifted = value if c == HALF else pltpu.roll(value, (HALF - c) % LANES, 1)
            high = shifted.astype(bf16)
            low = (shifted - high.astype(f32)).astype(bf16)
            rows = pl.ds((y * TS + c) * EXT, EXT)
            pst[rows, pl.ds(0, LANES)] = high
            pst[rows, pl.ds(LANES, LANES)] = low
    for step in (1, 2, 4, 8):
        total = total + pltpu.roll(total, LANES - step, 1)
    total = pltpu.roll(total, HALF, 1)
    for step in (1, 2, 4, 8):
        total = total + pltpu.roll(total, EXT - step, 0)
    scale = sharpness * lax.rsqrt(total[:ROWS] + epsilon)

    if gather:
        for k in range(1, n):
            pltpu.make_async_remote_copy(
                src_ref=sendbuf, dst_ref=slots.at[lax.rem(me + n - k, n)], send_sem=bsend.at[k],
                recv_sem=brecv.at[k], device_id={"gx": lax.rem(me + k, n)}, device_id_type=MESH).wait_recv()

    tile = (NT, LANES)
    zero = [[slots[i, :, pl.ds(h * LANES, LANES)] for h in range(2)] for i in range(TS)]
    acc = functools.reduce(jnp.add, [x for pair in zero for x in pair])
    mean = jnp.sum(acc, axis=1, keepdims=True) * (1.0 / TS**3)
    zero = [[x - mean for x in pair] for pair in zero]
    acc = functools.reduce(jnp.add, [x * x for pair in zero for x in pair])
    inv = lax.rsqrt(jnp.sum(acc, axis=1, keepdims=True) + epsilon)
    zero = [[x * inv for x in pair] for pair in zero]

    tl = lane_iota(tile)
    one = swap_high(zero)
    for bit, dist in ((2, 64), (1, 32), (0, 16)):
        one = swap_bit(one, bit, dist, tl)
    two = zero
    for bit, dist in ((3, 8), (2, 4), (1, 2), (0, 1)):
        two = swap_bit(two, bit, dist, tl)

    sub = lax.broadcasted_iota(jnp.int32, tile, 0)
    o = jnp.zeros(tile, jnp.int32)
    for t in range(NT):
        o = jnp.where(sub == t, orient[t], o)
    p = o >> 3
    bit0, bit1, bit2 = o & 1, (o >> 1) & 1, (o >> 2) & 1
    rows0 = (p == 2) | (p == 3)
    rows1 = (p == 0) | (p == 5)
    flip_b = jnp.where(rows0, bit0, jnp.where(rows1, bit1, bit2)) == 1
    flip_u = jnp.where(rows1, bit0, bit1)
    flip_v = jnp.where(rows0 | rows1, bit2, bit0)
    which = (1 - (p & 1)) * 4 + flip_u * 2 + flip_v
    picked = [[jnp.where(rows0, zero[i][h], jnp.where(rows1, one[i][h], two[i][h])) for h in range(2)]
              for i in range(TS)]
    picked = [[jnp.where(flip_b, picked[TS - 1 - i][h], picked[i][h]) for h in range(2)] for i in range(TS)]
    which = jnp.concatenate([which, which], axis=0)
    for i in range(0, TS, 2):
        for h in range(2):
            both = jnp.concatenate([picked[i][h], picked[i + 1][h]], axis=0)
            high = both.astype(bf16).astype(f32)
            low = both - high
            for g in range(8):
                cols = pl.ds(g * TS * TS + h * LANES, LANES)
                lhs[pl.ds(i * NT, 2 * NT), cols] = jnp.where(which == g, high, 0.0).astype(bf16)
                lhs[pl.ds(TS * NT + i * NT, 2 * NT), cols] = jnp.where(which == g, low, 0.0).astype(bf16)
    turned = jnp.dot(lhs[...], hot[...], preferred_element_type=f32)
    rot[...] = turned[:TS * NT] + turned[TS * NT:]

    def band(b, carry):
        for j in range(KB // LANES):
            first = b * NT if isinstance(b, int) else pl.multiple_of(b * NT, NT)
            lines = rot[pl.ds(first, NT), pl.ds(j * LANES, LANES)]
            for t in range(NT):
                line = jnp.broadcast_to(lines[t:t + 1], (ROWS, LANES))
                line = pltpu.roll(line, 0, 1, stride=1, stride_axis=0)
                high = line.astype(bf16)
                low = (line - high.astype(f32)).astype(bf16)
                start = (b - 1) * KB + j * LANES
                cols = pl.ds(start if isinstance(b, int) else pl.multiple_of(start, LANES), LANES)
                wst[pl.ds(t * ROWS, ROWS), cols] = high
                wst[pl.ds((NT + t) * ROWS, ROWS), cols] = low
        return carry

    lax.fori_loop(1, BY + 1, band, 0)

    weights = []
    for k in range(FIELDS):
        parts = [jnp.full((ROWS, LANES), counts[k * PER + i].astype(f32)) for i in range(PER)]
        whole = functools.reduce(jnp.add, parts)
        weights.append([x / whole for x in parts])
    ol = lane_iota((ROWS, LANES))
    half_m = NT * ROWS
    after = [None] * FIELDS
    for y in reversed(range(BY)):
        if y:
            band(TS - y, 0)
        res = jnp.dot(wst[:, pl.ds((BY - 1 - y) * KB, BY * KB)], pst[...], preferred_element_type=f32)
        numer = (res[:half_m, :LANES] + (res[:half_m, LANES:] + res[half_m:, :LANES])) + res[half_m:, LANES:]
        for k in range(FIELDS):
            value = None
            for i in range(PER):
                t = k * PER + i
                term = weights[k][i] * jnp.exp(numer[t * ROWS:(t + 1) * ROWS] * scale)
                value = term if value is None else value + term
            value = jnp.log(value)
            if y:
                value = pltpu.roll(value, LANES - TS * y, 1)
            if y < BY - 1:
                out[k, :, pl.ds(y * LANES, LANES)] = jnp.where(ol < BZ - TS * y, value, after[k])
            after[k] = value

    if gather:
        for copy in sends:
            copy.wait_send()

    @pl.when(has_right)
    def _():
        to_right.wait_send()

    @pl.when(has_left)
    def _():
        to_left.wait_send()


def local(n, volume, bank, orient, bank_id, counts):
    gather = bank.shape[1] == TS * TS
    if not gather:
        whole = lax.all_gather(bank, "gx", axis=1, tiled=True)[bank_id]
        bank = whole.reshape(NT, TS, TS * TS).transpose(1, 0, 2)
    hbm = pl.BlockSpec(memory_space=pltpu.HBM)
    vmem = pl.BlockSpec(memory_space=pltpu.VMEM)
    return pl.pallas_call(
        functools.partial(kernel, n, gather),
        out_shape=jax.ShapeDtypeStruct((FIELDS, ROWS, BY * BZ), f32),
        in_specs=[hbm] * 5,
        out_specs=vmem,
        scratch_shapes=[
            pltpu.SMEM((NT,), jnp.int32),
            pltpu.SMEM((NT,), jnp.int32),
            pltpu.SMEM((NT,), jnp.int32),
            pltpu.VMEM(volume.shape, f32),
            pltpu.VMEM(bank.shape, f32),
            pltpu.VMEM((NT, TS * TS), f32),
            pltpu.VMEM((TS, NT, TS * TS), f32),
            pltpu.VMEM((EXT, BY * BZ), f32),
            pltpu.VMEM((BY * KB, 2 * LANES), bf16),
            pltpu.VMEM((2 * NT * ROWS, (TS - 1) * KB), bf16),
            pltpu.VMEM((8 * TS * TS, KB), bf16),
            pltpu.VMEM((2 * TS * NT, 8 * TS * TS), bf16),
            pltpu.VMEM((TS * NT, KB), f32),
            pltpu.SemaphoreType.DMA((5,)),
            pltpu.SemaphoreType.DMA((TS,)),
            pltpu.SemaphoreType.DMA((TS,)),
            pltpu.SemaphoreType.DMA((2,)),
            pltpu.SemaphoreType.DMA((2,)),
        ],
        compiler_params=pltpu.CompilerParams(
            collective_id=0, has_side_effects=True, vmem_limit_bytes=64 * 1024 * 1024),
        cost_estimate=pl.CostEstimate(flops=4_000_000_000, bytes_accessed=400_000, transcendentals=200_000),
    )(orient, bank_id, counts, volume, bank)


def solution(mesh):
    in_specs = (P(("grp", "gx"), None), P(None, "gx"), P(), P(), P())
    out_specs = P(None, ("grp", "gx"), None)
    return jax.shard_map(functools.partial(local, mesh.shape["gx"]), mesh=mesh, in_specs=in_specs,
                         out_specs=out_specs, check_vma=False)
```

```python
import functools

import jax
import jax.numpy as jnp
from jax import lax
from jax.experimental import pallas as pl
from jax.experimental.pallas import tpu as pltpu
from jax.sharding import PartitionSpec as P

BY = 8
BZ = 112
TS = 16
NT = 8
FIELDS = 4
PER = NT // FIELDS
ROWS = 16
EXT = ROWS + TS
LANES = 128
KB = TS * EXT
HALF = TS // 2
MESH = pl.DeviceIdType.MESH

epsilon = 1e-05
sharpness = 80.0
f32 = jnp.float32
bf16 = jnp.bfloat16


def lane_iota(shape):
    return lax.broadcasted_iota(jnp.int32, shape, len(shape) - 1)


def swap_bit(tiles, bit, dist, lane):
    out = list(tiles)
    low = (lane & dist) == 0
    for i in range(TS):
        if i & (1 << bit):
            continue
        j = i | (1 << bit)
        for h in range(2):
            a, b = tiles[i][h], tiles[j][h]
            na = jnp.where(low, a, pltpu.roll(b, dist, 1))
            nb = jnp.where(low, pltpu.roll(a, LANES - dist, 1), b)
            out[i] = [na if g == h else out[i][g] for g in range(2)]
            out[j] = [nb if g == h else out[j][g] for g in range(2)]
    return out


def swap_high(tiles):
    out = [None] * TS
    for i in range(TS):
        top = i >> 3
        out[i] = [tiles[(i & 7) | (h << 3)][top] for h in range(2)]
    return out


def kernel(n, gather, orient_in, bank_id_in, counts_in, vol_in, bank_in, out, orient, bank_id, counts, vol, bank,
           sendbuf, slots, ext, pst, wst, hot, lhs, rot, fetch, bsend, brecv, hsend, hrecv):
    pairs = ((vol_in, vol), (bank_id_in, bank_id), (bank_in, bank), (orient_in, orient), (counts_in, counts))
    fetches = [pltpu.make_async_copy(src, dst, fetch.at[i]) for i, (src, dst) in enumerate(pairs)]
    for copy in fetches:
        copy.start()
    me = lax.axis_index("gx")
    has_left = me > 0
    has_right = me < n - 1
    left = jnp.maximum(me - 1, 0)
    right = jnp.minimum(me + 1, n - 1)

    barrier = pltpu.get_barrier_semaphore()
    if gather:
        for k in range(1, n):
            pl.semaphore_signal(barrier, inc=1, device_id={"gx": lax.rem(me + k, n)}, device_id_type=MESH)
    else:
        @pl.when(has_left)
        def _():
            pl.semaphore_signal(barrier, inc=1, device_id={"gx": left}, device_id_type=MESH)

        @pl.when(has_right)
        def _():
            pl.semaphore_signal(barrier, inc=1, device_id={"gx": right}, device_id_type=MESH)

    fetches[1].wait()
    fetches[2].wait()
    if gather:
        for t in range(NT):
            sendbuf[t:t + 1, :] = bank[pl.ds(bank_id[t], 1), :]
        slots[me] = sendbuf[...]
        pl.semaphore_wait(barrier, n - 1)
    else:
        slots[...] = bank[...]

        @pl.when(has_left)
        def _():
            pl.semaphore_wait(barrier, 1)

        @pl.when(has_right)
        def _():
            pl.semaphore_wait(barrier, 1)

    to_right = pltpu.make_async_remote_copy(
        src_ref=vol.at[pl.ds(ROWS - HALF, HALF)], dst_ref=ext.at[pl.ds(0, HALF)],
        send_sem=hsend.at[0], recv_sem=hrecv.at[0], device_id={"gx": right}, device_id_type=MESH)
    to_left = pltpu.make_async_remote_copy(
        src_ref=vol.at[pl.ds(0, HALF)], dst_ref=ext.at[pl.ds(HALF + ROWS, HALF)],
        send_sem=hsend.at[1], recv_sem=hrecv.at[1], device_id={"gx": left}, device_id_type=MESH)

    sends = []
    if gather:
        for k in sorted(range(1, n), key=lambda i: -min(i, n - i)):
            copy = pltpu.make_async_remote_copy(
                src_ref=sendbuf, dst_ref=slots.at[me], send_sem=bsend.at[k], recv_sem=brecv.at[k],
                device_id={"gx": lax.rem(me + k, n)}, device_id_type=MESH)
            copy.start()
            sends.append(copy)

    fetches[0].wait()

    @pl.when(has_right)
    def _():
        to_right.start()

    @pl.when(has_left)
    def _():
        to_left.start()

    fetches[3].wait()
    fetches[4].wait()
    ext[pl.ds(HALF, ROWS), :] = vol[...]

    @pl.when(jnp.logical_not(has_left))
    def _():
        ext[pl.ds(0, HALF), :] = jnp.zeros((HALF, BY * BZ), f32)

    @pl.when(jnp.logical_not(has_right))
    def _():
        ext[pl.ds(HALF + ROWS, HALF), :] = jnp.zeros((HALF, BY * BZ), f32)

    wide = (TS * TS, KB)
    lane = lane_iota((1, KB))
    c_of, a_of = lane >> 5, lane & 31
    row = lax.broadcasted_iota(jnp.int32, wide, 0)
    for g in range(8):
        u = a_of if g & 4 else c_of
        v = c_of if g & 4 else a_of
        u = (TS - 1 - u) if g & 2 else u
        v = (TS - 1 - v) if g & 1 else v
        source = jnp.where(a_of < TS, u * TS + v, -1)
        hot[pl.ds(g * TS * TS, TS * TS), :] = jnp.where(row == source, 1.0, 0.0).astype(bf16)

    @pl.when(has_left)
    def _():
        to_right.wait_recv()

    @pl.when(has_right)
    def _():
        to_left.wait_recv()

    zl = lane_iota((EXT, LANES))
    total = None
    for y in range(BY):
        if y == 0:
            value = ext[:, pl.ds(0, LANES)]
        else:
            value = pltpu.roll(ext[:, pl.ds((y - 1) * LANES, LANES)], TS * y, 1)
            if y < BY - 1:
                value = jnp.where(zl < TS * y, value, pltpu.roll(ext[:, pl.ds(y * LANES, LANES)], TS * y, 1))
        value = jnp.where(zl < BZ, value, 0.0)
        square = value * value
        total = square if total is None else total + square
        for c in range(TS):
            shifted = value if c == HALF else pltpu.roll(value, (HALF - c) % LANES, 1)
            high = shifted.astype(bf16)
            low = (shifted - high.astype(f32)).astype(bf16)
            rows = pl.ds((y * TS + c) * EXT, EXT)
            pst[rows, pl.ds(0, LANES)] = high
            pst[rows, pl.ds(LANES, LANES)] = low
    for step in (1, 2, 4, 8):
        total = total + pltpu.roll(total, LANES - step, 1)
    total = pltpu.roll(total, HALF, 1)
    for step in (1, 2, 4, 8):
        total = total + pltpu.roll(total, EXT - step, 0)
    scale = sharpness * lax.rsqrt(total[:ROWS] + epsilon)

    if gather:
        for k in range(1, n):
            pltpu.make_async_remote_copy(
                src_ref=sendbuf, dst_ref=slots.at[lax.rem(me + n - k, n)], send_sem=bsend.at[k],
                recv_sem=brecv.at[k], device_id={"gx": lax.rem(me + k, n)}, device_id_type=MESH).wait_recv()

    tile = (NT, LANES)
    zero = [[slots[i, :, pl.ds(h * LANES, LANES)] for h in range(2)] for i in range(TS)]
    acc = functools.reduce(jnp.add, [x for pair in zero for x in pair])
    mean = jnp.sum(acc, axis=1, keepdims=True) * (1.0 / TS**3)
    zero = [[x - mean for x in pair] for pair in zero]
    acc = functools.reduce(jnp.add, [x * x for pair in zero for x in pair])
    inv = lax.rsqrt(jnp.sum(acc, axis=1, keepdims=True) + epsilon)
    zero = [[x * inv for x in pair] for pair in zero]

    tl = lane_iota(tile)
    one = swap_high(zero)
    for bit, dist in ((2, 64), (1, 32), (0, 16)):
        one = swap_bit(one, bit, dist, tl)
    two = zero
    for bit, dist in ((3, 8), (2, 4), (1, 2), (0, 1)):
        two = swap_bit(two, bit, dist, tl)

    sub = lax.broadcasted_iota(jnp.int32, tile, 0)
    o = jnp.zeros(tile, jnp.int32)
    for t in range(NT):
        o = jnp.where(sub == t, orient[t], o)
    p = o >> 3
    bit0, bit1, bit2 = o & 1, (o >> 1) & 1, (o >> 2) & 1
    rows0 = (p == 2) | (p == 3)
    rows1 = (p == 0) | (p == 5)
    flip_b = jnp.where(rows0, bit0, jnp.where(rows1, bit1, bit2)) == 1
    flip_u = jnp.where(rows1, bit0, bit1)
    flip_v = jnp.where(rows0 | rows1, bit2, bit0)
    which = (1 - (p & 1)) * 4 + flip_u * 2 + flip_v
    picked = [[jnp.where(rows0, zero[i][h], jnp.where(rows1, one[i][h], two[i][h])) for h in range(2)]
              for i in range(TS)]
    picked = [[jnp.where(flip_b, picked[TS - 1 - i][h], picked[i][h]) for h in range(2)] for i in range(TS)]
    which = jnp.concatenate([which, which], axis=0)
    for i in range(0, TS, 2):
        for h in range(2):
            both = jnp.concatenate([picked[i][h], picked[i + 1][h]], axis=0)
            high = both.astype(bf16).astype(f32)
            low = both - high
            for g in range(8):
                cols = pl.ds(g * TS * TS + h * LANES, LANES)
                lhs[pl.ds(i * NT, 2 * NT), cols] = jnp.where(which == g, high, 0.0).astype(bf16)
                lhs[pl.ds(TS * NT + i * NT, 2 * NT), cols] = jnp.where(which == g, low, 0.0).astype(bf16)
    turned = jnp.dot(lhs[...], hot[...], preferred_element_type=f32)
    rot[...] = turned[:TS * NT] + turned[TS * NT:]

    def band(b, carry):
        for j in range(KB // LANES):
            first = b * NT if isinstance(b, int) else pl.multiple_of(b * NT, NT)
            lines = rot[pl.ds(first, NT), pl.ds(j * LANES, LANES)]
            for t in range(NT):
                line = jnp.broadcast_to(lines[t:t + 1], (ROWS, LANES))
                line = pltpu.roll(line, 0, 1, stride=1, stride_axis=0)
                high = line.astype(bf16)
                low = (line - high.astype(f32)).astype(bf16)
                start = (b - 1) * KB + j * LANES
                cols = pl.ds(start if isinstance(b, int) else pl.multiple_of(start, LANES), LANES)
                wst[pl.ds(t * ROWS, ROWS), cols] = high
                wst[pl.ds((NT + t) * ROWS, ROWS), cols] = low
        return carry

    lax.fori_loop(1, BY + 1, band, 0)

    weights = []
    for k in range(FIELDS):
        parts = [jnp.full((ROWS, LANES), counts[k * PER + i].astype(f32)) for i in range(PER)]
        whole = functools.reduce(jnp.add, parts)
        weights.append([x / whole for x in parts])
    ol = lane_iota((ROWS, LANES))
    half_m = NT * ROWS
    after = [None] * FIELDS
    for y in reversed(range(BY)):
        if y:
            band(TS - y, 0)
        res = jnp.dot(wst[:, pl.ds((BY - 1 - y) * KB, BY * KB)], pst[...], preferred_element_type=f32)
        numer = (res[:half_m, :LANES] + (res[:half_m, LANES:] + res[half_m:, :LANES])) + res[half_m:, LANES:]
        for k in range(FIELDS):
            value = None
            for i in range(PER):
                t = k * PER + i
                term = weights[k][i] * jnp.exp(numer[t * ROWS:(t + 1) * ROWS] * scale)
                value = term if value is None else value + term
            value = jnp.log(value)
            if y:
                value = pltpu.roll(value, LANES - TS * y, 1)
            if y < BY - 1:
                out[k, :, pl.ds(y * LANES, LANES)] = jnp.where(ol < BZ - TS * y, value, after[k])
            after[k] = value

    if gather:
        for copy in sends:
            copy.wait_send()

    @pl.when(has_right)
    def _():
        to_right.wait_send()

    @pl.when(has_left)
    def _():
        to_left.wait_send()


def local(n, volume, bank, orient, bank_id, counts):
    gather = bank.shape[1] == TS * TS
    if not gather:
        whole = lax.all_gather(bank, "gx", axis=1, tiled=True)[bank_id]
        bank = whole.reshape(NT, TS, TS * TS).transpose(1, 0, 2)
    hbm = pl.BlockSpec(memory_space=pltpu.HBM)
    vmem = pl.BlockSpec(memory_space=pltpu.VMEM)
    return pl.pallas_call(
        functools.partial(kernel, n, gather),
        out_shape=jax.ShapeDtypeStruct((FIELDS, ROWS, BY * BZ), f32),
        in_specs=[hbm] * 5,
        out_specs=vmem,
        scratch_shapes=[
            pltpu.SMEM((NT,), jnp.int32),
            pltpu.SMEM((NT,), jnp.int32),
            pltpu.SMEM((NT,), jnp.int32),
            pltpu.VMEM(volume.shape, f32),
            pltpu.VMEM(bank.shape, f32),
            pltpu.VMEM((NT, TS * TS), f32),
            pltpu.VMEM((TS, NT, TS * TS), f32),
            pltpu.VMEM((EXT, BY * BZ), f32),
            pltpu.VMEM((BY * KB, 2 * LANES), bf16),
            pltpu.VMEM((2 * NT * ROWS, (TS - 1) * KB), bf16),
            pltpu.VMEM((8 * TS * TS, KB), bf16),
            pltpu.VMEM((2 * TS * NT, 8 * TS * TS), bf16),
            pltpu.VMEM((TS * NT, KB), f32),
            pltpu.SemaphoreType.DMA((5,)),
            pltpu.SemaphoreType.DMA((TS,)),
            pltpu.SemaphoreType.DMA((TS,)),
            pltpu.SemaphoreType.DMA((2,)),
            pltpu.SemaphoreType.DMA((2,)),
        ],
        compiler_params=pltpu.CompilerParams(
            collective_id=0, has_side_effects=True, vmem_limit_bytes=64 * 1024 * 1024),
        cost_estimate=pl.CostEstimate(flops=4_000_000_000, bytes_accessed=400_000, transcendentals=200_000),
    )(orient, bank_id, counts, volume, bank)


def solution(mesh):
    in_specs = (P(("grp", "gx"), None), P(None, "gx"), P(), P(), P())
    out_specs = P(None, ("grp", "gx"), None)
    return jax.shard_map(functools.partial(local, mesh.shape["gx"]), mesh=mesh, in_specs=in_specs,
                         out_specs=out_specs, check_vma=False)
```

```python
import functools

import jax
import jax.numpy as jnp
from jax import lax
from jax.experimental import pallas as pl
from jax.experimental.pallas import tpu as pltpu
from jax.sharding import PartitionSpec as P

BY = 8
BZ = 112
TS = 16
NT = 8
FIELDS = 4
PER = NT // FIELDS
ROWS = 16
EXT = ROWS + TS
LANES = 128
KB = TS * EXT
HALF = TS // 2
MESH = pl.DeviceIdType.MESH

epsilon = 1e-05
sharpness = 80.0
f32 = jnp.float32
bf16 = jnp.bfloat16


def lane_iota(shape):
    return lax.broadcasted_iota(jnp.int32, shape, len(shape) - 1)


def swap_bit(tiles, bit, dist, lane):
    out = list(tiles)
    low = (lane & dist) == 0
    for i in range(TS):
        if i & (1 << bit):
            continue
        j = i | (1 << bit)
        for h in range(2):
            a, b = tiles[i][h], tiles[j][h]
            na = jnp.where(low, a, pltpu.roll(b, dist, 1))
            nb = jnp.where(low, pltpu.roll(a, LANES - dist, 1), b)
            out[i] = [na if g == h else out[i][g] for g in range(2)]
            out[j] = [nb if g == h else out[j][g] for g in range(2)]
    return out


def swap_high(tiles):
    out = [None] * TS
    for i in range(TS):
        top = i >> 3
        out[i] = [tiles[(i & 7) | (h << 3)][top] for h in range(2)]
    return out


def kernel(n, gather, orient_in, bank_id_in, counts_in, vol_in, bank_in, out, orient, bank_id, counts, vol, bank,
           sendbuf, slots, ext, pst, wst, hot, lhs, rot, fetch, bsend, brecv, hsend, hrecv):
    pairs = ((vol_in, vol), (bank_id_in, bank_id), (bank_in, bank), (orient_in, orient), (counts_in, counts))
    fetches = [pltpu.make_async_copy(src, dst, fetch.at[i]) for i, (src, dst) in enumerate(pairs)]
    for copy in fetches:
        copy.start()
    me = lax.axis_index("gx")
    has_left = me > 0
    has_right = me < n - 1
    left = jnp.maximum(me - 1, 0)
    right = jnp.minimum(me + 1, n - 1)

    barrier = pltpu.get_barrier_semaphore()
    if gather:
        for k in range(1, n):
            pl.semaphore_signal(barrier, inc=1, device_id={"gx": lax.rem(me + k, n)}, device_id_type=MESH)
    else:
        @pl.when(has_left)
        def _():
            pl.semaphore_signal(barrier, inc=1, device_id={"gx": left}, device_id_type=MESH)

        @pl.when(has_right)
        def _():
            pl.semaphore_signal(barrier, inc=1, device_id={"gx": right}, device_id_type=MESH)

    fetches[1].wait()
    fetches[2].wait()
    if gather:
        for t in range(NT):
            sendbuf[t:t + 1, :] = bank[pl.ds(bank_id[t], 1), :]
        slots[me] = sendbuf[...]
        pl.semaphore_wait(barrier, n - 1)
    else:
        slots[...] = bank[...]

        @pl.when(has_left)
        def _():
            pl.semaphore_wait(barrier, 1)

        @pl.when(has_right)
        def _():
            pl.semaphore_wait(barrier, 1)

    to_right = pltpu.make_async_remote_copy(
        src_ref=vol.at[pl.ds(ROWS - HALF, HALF)], dst_ref=ext.at[pl.ds(0, HALF)],
        send_sem=hsend.at[0], recv_sem=hrecv.at[0], device_id={"gx": right}, device_id_type=MESH)
    to_left = pltpu.make_async_remote_copy(
        src_ref=vol.at[pl.ds(0, HALF)], dst_ref=ext.at[pl.ds(HALF + ROWS, HALF)],
        send_sem=hsend.at[1], recv_sem=hrecv.at[1], device_id={"gx": left}, device_id_type=MESH)

    sends = []
    if gather:
        for k in sorted(range(1, n), key=lambda i: -min(i, n - i)):
            copy = pltpu.make_async_remote_copy(
                src_ref=sendbuf, dst_ref=slots.at[me], send_sem=bsend.at[k], recv_sem=brecv.at[k],
                device_id={"gx": lax.rem(me + k, n)}, device_id_type=MESH)
            copy.start()
            sends.append(copy)

    fetches[0].wait()

    @pl.when(has_right)
    def _():
        to_right.start()

    @pl.when(has_left)
    def _():
        to_left.start()

    fetches[3].wait()
    fetches[4].wait()
    ext[pl.ds(HALF, ROWS), :] = vol[...]

    @pl.when(jnp.logical_not(has_left))
    def _():
        ext[pl.ds(0, HALF), :] = jnp.zeros((HALF, BY * BZ), f32)

    @pl.when(jnp.logical_not(has_right))
    def _():
        ext[pl.ds(HALF + ROWS, HALF), :] = jnp.zeros((HALF, BY * BZ), f32)

    wide = (TS * TS, KB)
    lane = lane_iota((1, KB))
    c_of, a_of = lane >> 5, lane & 31
    row = lax.broadcasted_iota(jnp.int32, wide, 0)
    for g in range(8):
        u = a_of if g & 4 else c_of
        v = c_of if g & 4 else a_of
        u = (TS - 1 - u) if g & 2 else u
        v = (TS - 1 - v) if g & 1 else v
        source = jnp.where(a_of < TS, u * TS + v, -1)
        hot[pl.ds(g * TS * TS, TS * TS), :] = jnp.where(row == source, 1.0, 0.0).astype(bf16)

    @pl.when(has_left)
    def _():
        to_right.wait_recv()

    @pl.when(has_right)
    def _():
        to_left.wait_recv()

    zl = lane_iota((EXT, LANES))
    total = None
    for y in range(BY):
        if y == 0:
            value = ext[:, pl.ds(0, LANES)]
        else:
            value = pltpu.roll(ext[:, pl.ds((y - 1) * LANES, LANES)], TS * y, 1)
            if y < BY - 1:
                value = jnp.where(zl < TS * y, value, pltpu.roll(ext[:, pl.ds(y * LANES, LANES)], TS * y, 1))
        value = jnp.where(zl < BZ, value, 0.0)
        square = value * value
        total = square if total is None else total + square
        for c in range(TS):
            shifted = value if c == HALF else pltpu.roll(value, (HALF - c) % LANES, 1)
            high = shifted.astype(bf16)
            low = (shifted - high.astype(f32)).astype(bf16)
            rows = pl.ds((y * TS + c) * EXT, EXT)
            pst[rows, pl.ds(0, LANES)] = high
            pst[rows, pl.ds(LANES, LANES)] = low
    for step in (1, 2, 4, 8):
        total = total + pltpu.roll(total, LANES - step, 1)
    total = pltpu.roll(total, HALF, 1)
    for step in (1, 2, 4, 8):
        total = total + pltpu.roll(total, EXT - step, 0)
    scale = sharpness * lax.rsqrt(total[:ROWS] + epsilon)

    if gather:
        for k in range(1, n):
            pltpu.make_async_remote_copy(
                src_ref=sendbuf, dst_ref=slots.at[lax.rem(me + n - k, n)], send_sem=bsend.at[k],
                recv_sem=brecv.at[k], device_id={"gx": lax.rem(me + k, n)}, device_id_type=MESH).wait_recv()

    tile = (NT, LANES)
    zero = [[slots[i, :, pl.ds(h * LANES, LANES)] for h in range(2)] for i in range(TS)]
    acc = functools.reduce(jnp.add, [x for pair in zero for x in pair])
    mean = jnp.sum(acc, axis=1, keepdims=True) * (1.0 / TS**3)
    zero = [[x - mean for x in pair] for pair in zero]
    acc = functools.reduce(jnp.add, [x * x for pair in zero for x in pair])
    inv = lax.rsqrt(jnp.sum(acc, axis=1, keepdims=True) + epsilon)
    zero = [[x * inv for x in pair] for pair in zero]

    tl = lane_iota(tile)
    one = swap_high(zero)
    for bit, dist in ((2, 64), (1, 32), (0, 16)):
        one = swap_bit(one, bit, dist, tl)
    two = zero
    for bit, dist in ((3, 8), (2, 4), (1, 2), (0, 1)):
        two = swap_bit(two, bit, dist, tl)

    sub = lax.broadcasted_iota(jnp.int32, tile, 0)
    o = jnp.zeros(tile, jnp.int32)
    for t in range(NT):
        o = jnp.where(sub == t, orient[t], o)
    p = o >> 3
    bit0, bit1, bit2 = o & 1, (o >> 1) & 1, (o >> 2) & 1
    rows0 = (p == 2) | (p == 3)
    rows1 = (p == 0) | (p == 5)
    flip_b = jnp.where(rows0, bit0, jnp.where(rows1, bit1, bit2)) == 1
    flip_u = jnp.where(rows1, bit0, bit1)
    flip_v = jnp.where(rows0 | rows1, bit2, bit0)
    which = (1 - (p & 1)) * 4 + flip_u * 2 + flip_v
    picked = [[jnp.where(rows0, zero[i][h], jnp.where(rows1, one[i][h], two[i][h])) for h in range(2)]
              for i in range(TS)]
    picked = [[jnp.where(flip_b, picked[TS - 1 - i][h], picked[i][h]) for h in range(2)] for i in range(TS)]
    which = jnp.concatenate([which, which], axis=0)
    for i in range(0, TS, 2):
        for h in range(2):
            both = jnp.concatenate([picked[i][h], picked[i + 1][h]], axis=0)
            high = both.astype(bf16).astype(f32)
            low = both - high
            for g in range(8):
                cols = pl.ds(g * TS * TS + h * LANES, LANES)
                lhs[pl.ds(i * NT, 2 * NT), cols] = jnp.where(which == g, high, 0.0).astype(bf16)
                lhs[pl.ds(TS * NT + i * NT, 2 * NT), cols] = jnp.where(which == g, low, 0.0).astype(bf16)
    turned = jnp.dot(lhs[...], hot[...], preferred_element_type=f32)
    rot[...] = turned[:TS * NT] + turned[TS * NT:]

    def band(b, carry):
        for j in range(KB // LANES):
            first = b * NT if isinstance(b, int) else pl.multiple_of(b * NT, NT)
            lines = rot[pl.ds(first, NT), pl.ds(j * LANES, LANES)]
            for t in range(NT):
                line = jnp.broadcast_to(lines[t:t + 1], (ROWS, LANES))
                line = pltpu.roll(line, 0, 1, stride=1, stride_axis=0)
                high = line.astype(bf16)
                low = (line - high.astype(f32)).astype(bf16)
                start = (b - 1) * KB + j * LANES
                cols = pl.ds(start if isinstance(b, int) else pl.multiple_of(start, LANES), LANES)
                wst[pl.ds(t * ROWS, ROWS), cols] = high
                wst[pl.ds((NT + t) * ROWS, ROWS), cols] = low
        return carry

    for b in range(1, BY + 1):
        band(b, 0)

    weights = []
    for k in range(FIELDS):
        parts = [jnp.full((ROWS, LANES), counts[k * PER + i].astype(f32)) for i in range(PER)]
        whole = functools.reduce(jnp.add, parts)
        weights.append([x / whole for x in parts])
    ol = lane_iota((ROWS, LANES))
    half_m = NT * ROWS
    after = [None] * FIELDS
    for y in reversed(range(BY)):
        if y:
            band(TS - y, 0)
        res = jnp.dot(wst[:, pl.ds((BY - 1 - y) * KB, BY * KB)], pst[...], preferred_element_type=f32)
        numer = (res[:half_m, :LANES] + (res[:half_m, LANES:] + res[half_m:, :LANES])) + res[half_m:, LANES:]
        for k in range(FIELDS):
            value = None
            for i in range(PER):
                t = k * PER + i
                term = weights[k][i] * jnp.exp(numer[t * ROWS:(t + 1) * ROWS] * scale)
                value = term if value is None else value + term
            value = jnp.log(value)
            if y:
                value = pltpu.roll(value, LANES - TS * y, 1)
            if y < BY - 1:
                out[k, :, pl.ds(y * LANES, LANES)] = jnp.where(ol < BZ - TS * y, value, after[k])
            after[k] = value

    if gather:
        for copy in sends:
            copy.wait_send()

    @pl.when(has_right)
    def _():
        to_right.wait_send()

    @pl.when(has_left)
    def _():
        to_left.wait_send()


def local(n, volume, bank, orient, bank_id, counts):
    gather = bank.shape[1] == TS * TS
    if not gather:
        whole = lax.all_gather(bank, "gx", axis=1, tiled=True)[bank_id]
        bank = whole.reshape(NT, TS, TS * TS).transpose(1, 0, 2)
    hbm = pl.BlockSpec(memory_space=pltpu.HBM)
    vmem = pl.BlockSpec(memory_space=pltpu.VMEM)
    return pl.pallas_call(
        functools.partial(kernel, n, gather),
        out_shape=jax.ShapeDtypeStruct((FIELDS, ROWS, BY * BZ), f32),
        in_specs=[hbm] * 5,
        out_specs=vmem,
        scratch_shapes=[
            pltpu.SMEM((NT,), jnp.int32),
            pltpu.SMEM((NT,), jnp.int32),
            pltpu.SMEM((NT,), jnp.int32),
            pltpu.VMEM(volume.shape, f32),
            pltpu.VMEM(bank.shape, f32),
            pltpu.VMEM((NT, TS * TS), f32),
            pltpu.VMEM((TS, NT, TS * TS), f32),
            pltpu.VMEM((EXT, BY * BZ), f32),
            pltpu.VMEM((BY * KB, 2 * LANES), bf16),
            pltpu.VMEM((2 * NT * ROWS, (TS - 1) * KB), bf16),
            pltpu.VMEM((8 * TS * TS, KB), bf16),
            pltpu.VMEM((2 * TS * NT, 8 * TS * TS), bf16),
            pltpu.VMEM((TS * NT, KB), f32),
            pltpu.SemaphoreType.DMA((5,)),
            pltpu.SemaphoreType.DMA((TS,)),
            pltpu.SemaphoreType.DMA((TS,)),
            pltpu.SemaphoreType.DMA((2,)),
            pltpu.SemaphoreType.DMA((2,)),
        ],
        compiler_params=pltpu.CompilerParams(
            collective_id=0, has_side_effects=True, vmem_limit_bytes=64 * 1024 * 1024),
        cost_estimate=pl.CostEstimate(flops=4_000_000_000, bytes_accessed=400_000, transcendentals=200_000),
    )(orient, bank_id, counts, volume, bank)


def solution(mesh):
    in_specs = (P(("grp", "gx"), None), P(None, "gx"), P(), P(), P())
    out_specs = P(None, ("grp", "gx"), None)
    return jax.shard_map(functools.partial(local, mesh.shape["gx"]), mesh=mesh, in_specs=in_specs,
                         out_specs=out_specs, check_vma=False)
```
